32 devices in a mesh: up: 8 (over z, y), down: 4 (over x, core).
Axes of the slice: x: 2, y: 2, z: 4, core: 2. Of those that a mesh axis runs over, the one named last changes fastest.
Arguments:
- amplitudes: float32 [4096, 4096], P('up', 'down'), may hold values from -6 to 6
- double_occ: int32 [4096, 4096], P('up', 'down'), may hold values from 0 to 8
- up_cols: int32 [64, 32], replicated, may hold values from 0 to 63, as said below
- up_ids: int32 [64, 32], replicated, may hold values from 0 to 31, as said below
- up_blocks: bfloat16 [32, 64, 64], replicated, may hold values from -0.125 to 0.125
- down_cols: int32 [64, 32], replicated, may hold values from 0 to 63, as said below
- down_ids: int32 [64, 32], replicated, may hold values from 0 to 31, as said below
- down_blocks: bfloat16 [32, 64, 64], replicated, may hold values from -0.125 to 0.125
Outputs:
- chebyshev: float32 [4096, 4096], P('up', 'down')
The draws below stay inside these ranges and needn't reach their ends.
Inputs may be any that keep to these rules, and one draw needn't show every extreme that they name: `up_cols`: each row names 32 different blocks. `up_ids`: each row names every shared block exactly once. `down_cols`: each row names 32 different blocks. `down_ids`: each row names every shared block exactly once.
All inputs are finite; a program needn't handle non-finite values.
Results may differ from the reference program's by a relative error of at most 0.0031.
Values may be sent and summed in bfloat16 or wider, within the bound.
A program may use at most 128 MiB of HBM per device.

```python
import jax
import jax.numpy as jnp
from jax import lax

BLK = 64
NBLK = 64
BPR = 32
NSTR = 4096


def pattern_cols(key):

    def one_row(row_key):
        return jax.random.permutation(row_key, NBLK).astype(jnp.int32)
    orders = jax.vmap(one_row)(jax.random.split(key, NBLK))
    rank_table = jnp.argsort(orders, axis=1, stable=True).astype(jnp.int32)
    blocks_all = jnp.arange(NBLK, dtype=jnp.int32)
    end_blocks = (blocks_all == 0) | (blocks_all == NBLK - 1)
    scores = jnp.where(end_blocks, -1, rank_table[0])
    chosen = jnp.argsort(scores, stable=True).astype(jnp.int32)[:BPR]
    return orders[:, :BPR].at[0].set(chosen).astype(jnp.int32)


def pattern_ids(key):

    def one_row(row_key):
        return jax.random.permutation(row_key, BPR).astype(jnp.int32)
    return jax.vmap(one_row)(jax.random.split(key, NBLK)).astype(jnp.int32)


def draw_up_cols(key, part):
    return pattern_cols(jax.random.fold_in(key, 11))


def draw_down_cols(key, part):
    return pattern_cols(jax.random.fold_in(key, 23))


def draw_up_ids(key, part):
    return pattern_ids(jax.random.fold_in(key, 31))


def draw_down_ids(key, part):
    return pattern_ids(jax.random.fold_in(key, 47))


def plant(entries, own_key, least, high):
    extent = entries.shape
    place = [jax.random.randint(jax.random.fold_in(own_key, axis), (), 0, extent[axis]) for axis in range(len(extent))]
    entries = entries.at[tuple(place)].set(least)
    longest = extent.index(max(extent))
    place[longest] = (place[longest] + 1) % extent[longest]
    return entries.at[tuple(place)].set(high)


def levels(own_key, dims, cuts, low, largest):
    loudness, own = 1.0, jax.random.fold_in(own_key, 6)
    for position, parts in cuts:
        steps = jnp.exp(jax.random.uniform(jax.random.fold_in(own, position), (parts,), jnp.float32, low / len(cuts), largest / len(cuts)))
        loudness = loudness * jnp.repeat(steps, dims[position] // parts).reshape([-1 if axis == position else 1 for axis in range(len(dims))])
    return loudness


def bell_draw(key, dims, width, reach, cuts=(), kind=jnp.bfloat16):
    loudness = levels(key, dims, cuts, -0.22, 0.18) if cuts else 1.0
    entries = jax.random.normal(key, dims, jnp.float32) * width * loudness
    return jnp.minimum(jnp.maximum(entries, -reach), reach).astype(kind)


def setup_inputs(seed: int = 0) -> dict:
    keys = jax.random.split(jax.random.key(seed), 9)
    amplitudes = bell_draw(keys[0], (NSTR, NSTR), 1.0, 6.0, ((0, 8), (1, 4)), jnp.float32)
    double_occ = plant(jax.random.randint(keys[1], (NSTR, NSTR), 0, 9), jax.random.fold_in(keys[1], 1), 0, 8).astype(jnp.int32)
    up_cols = draw_up_cols(jax.random.fold_in(keys[8], 71), 0)
    up_ids = draw_up_ids(jax.random.fold_in(keys[8], 71), 0)
    up_blocks = bell_draw(keys[4], (BPR, BLK, BLK), (BPR * BLK) ** -0.5, 0.125)
    down_cols = draw_down_cols(jax.random.fold_in(keys[8], 71), 0)
    down_ids = draw_down_ids(jax.random.fold_in(keys[8], 71), 0)
    down_blocks = bell_draw(keys[7], (BPR, BLK, BLK), (BPR * BLK) ** -0.5, 0.125)
    return dict(amplitudes=amplitudes, double_occ=double_occ, up_cols=up_cols, up_ids=up_ids, up_blocks=up_blocks, down_cols=down_cols, down_ids=down_ids, down_blocks=down_blocks)


coupling = 0.5
center = 2.0
half_span = 2.0


def hop_last(values, block_cols, block_ids, shared_table):
    row_count = values.shape[0]
    block_width = shared_table.shape[1]
    block_total = values.shape[1] // block_width
    pieces = values.astype(jnp.float32).reshape(row_count, block_total, block_width)
    wide_table = shared_table.astype(jnp.float32)

    def one_block(row_pattern):
        row_cols, row_ids = row_pattern
        taken_rows = jnp.take(pieces, row_cols.astype(jnp.int32), axis=1)
        weights = jnp.take(wide_table, row_ids.astype(jnp.int32), axis=0)
        return jnp.einsum("ckb,kba->ca", taken_rows, weights, precision=lax.Precision.HIGHEST)

    outputs = lax.map(one_block, (block_cols, block_ids))
    return jnp.transpose(outputs, (1, 0, 2)).reshape(row_count, block_total * block_width)


def reference(amplitudes, double_occ, up_cols, up_ids, up_blocks, down_cols, down_ids, down_blocks):
    onsite = coupling * double_occ.astype(jnp.float32) - center

    def apply_scaled(current):
        rounded = lax.optimization_barrier(current.astype(jnp.bfloat16))
        up_hop = hop_last(rounded.T, up_cols, up_ids, up_blocks).T
        down_hop = hop_last(rounded, down_cols, down_ids, down_blocks)
        return (onsite * current + up_hop + down_hop) / half_span

    first = apply_scaled(amplitudes)
    return 2.0 * apply_scaled(first) - amplitudes
```

```python
import functools
import math

import jax
import jax.numpy as jnp
from jax import lax
from jax.experimental import pallas as pl
from jax.experimental.pallas import tpu as pltpu
from jax.sharding import PartitionSpec as P

coupling = 0.5
center = 2.0
LANES = 128
MESH = pl.DeviceIdType.MESH
F32 = jnp.float32
BF16 = jnp.bfloat16


def kernel(dims, up_map, down_map, amp, occ, up_tab, down_tab, out,
           tup, tdn, gath, vbuf, ret_out, ret_in, dsum, first,
           zs, zr, ys, yr, rs, rr, xs, xr, cs, cr):
    A, B, X, C, R, blk = dims
    DN = 2 * X
    u = lax.axis_index("up")
    d = lax.axis_index("down")
    me_a, me_b = lax.div(u, B), lax.rem(u, B)
    me_x, me_k = lax.div(d, 2), lax.rem(d, 2)
    AW = A * LANES
    sends = []

    def at_a(da):
        return lax.rem(me_a + da + A, A)

    def at_b(db):
        return lax.rem(me_b + db + B, B)

    def at_x(dx):
        return lax.rem(me_x + dx + X, X)

    def start(src, dst, ssem, rsem, dev):
        copy = pltpu.make_async_remote_copy(
            src_ref=src, dst_ref=dst, send_sem=ssem, recv_sem=rsem,
            device_id=dev, device_id_type=MESH)
        copy.start()
        sends.append(copy)

    def arrived(ref, ssem, rsem, dev):
        pltpu.make_async_remote_copy(
            src_ref=ref, dst_ref=ref, send_sem=ssem, recv_sem=rsem,
            device_id=dev, device_id_type=MESH).wait_recv()

    def forward_y(s, c, da):
        piece = vbuf.at[s, c, at_a(-da), me_b]
        for db in range(1, B):
            start(piece, piece, ys.at[s, c, da, db], yr.at[s, c, da, db],
                  (me_a * B + at_b(db), d))

    def forward_core(s, c, dx):
        piece = gath.at[s, at_x(-dx) * 2 + me_k, c]
        start(piece, piece, cs.at[s, c, dx], cr.at[s, c, dx], (u, me_x * 2 + 1 - me_k))

    def send_z(s, c):
        for da in z_order:
            start(gath.at[s, d, c, at_a(da)], vbuf.at[s, c, me_a, me_b],
                  zs.at[s, c, da], zr.at[s, c, da], (at_a(da) * B + me_b, d))
        vbuf[s, c, me_a, me_b] = gath[s, d, c, me_a]
        forward_y(s, c, 0)

    def send_down(s, c):
        for dx in range(1, X):
            piece = gath.at[s, d, c]
            start(piece, piece, xs.at[s, c, dx], xr.at[s, c, dx], (u, at_x(dx) * 2 + me_k))
        forward_core(s, c, 0)

    def take_z(s, c):
        for da in range(1, A):
            arrived(vbuf.at[s, c, at_a(-da), me_b], zs.at[s, c, da], zr.at[s, c, da],
                    (at_a(-da) * B + me_b, d))
            forward_y(s, c, da)

    def take_x(s, c):
        for dx in range(1, X):
            arrived(gath.at[s, at_x(-dx) * 2 + me_k, c], xs.at[s, c, dx], xr.at[s, c, dx],
                    (u, at_x(-dx) * 2 + me_k))
            forward_core(s, c, dx)

    def take_y(s, c):
        for da in range(A):
            for db in range(1, B):
                arrived(vbuf.at[s, c, at_a(-da), at_b(-db)], ys.at[s, c, da, db],
                        yr.at[s, c, da, db], (me_a * B + at_b(-db), d))

    def take_core(s, c):
        for dx in range(X):
            arrived(gath.at[s, at_x(-dx) * 2 + 1 - me_k, c], cs.at[s, c, dx], cr.at[s, c, dx],
                    (u, me_x * 2 + 1 - me_k))

    z_order = [A // 2] + [da for da in range(1, A) if da != A // 2]
    step_rows = math.gcd(R, 256)

    def up_hop(s, c):
        for da in z_order + [0]:
            dest = at_a(da)
            put = ret_in.at[s, c, me_a] if da == 0 else ret_out.at[s, c, da]

            def rows(i, _):
                base = pl.multiple_of(i * step_rows, step_rows)
                left = tup[dest, pl.ds(base, step_rows), :]
                right = vbuf[s, c].reshape(A * B * R, LANES)
                put[pl.ds(base, step_rows), :] = jnp.dot(
                    left, right, preferred_element_type=F32).astype(BF16)
                return 0

            lax.fori_loop(0, R // step_rows, rows, 0)
            if da:
                start(put, ret_in.at[s, c, me_a], rs.at[s, c, da], rr.at[s, c, da],
                      (dest * B + me_b, d))

    def take_ret(s, c):
        for da in range(1, A):
            arrived(ret_in.at[s, c, at_a(-da)], rs.at[s, c, da], rr.at[s, c, da],
                    (at_a(-da) * B + me_b, d))

    def down_hop(s):
        dsum[...] = jnp.zeros_like(dsum)
        per_n = 256
        for c in range(C):
            def part(i, _):
                src = lax.div(i, C * AW // per_n)
                col = pl.multiple_of(lax.rem(i, C * AW // per_n) * per_n, per_n)
                left = jnp.concatenate([gath[s, src, c, a] for a in range(A)], axis=1)
                k0 = pl.multiple_of((src * C + c) * AW, AW)
                dsum[:, pl.ds(col, per_n)] += jnp.dot(
                    left, tdn[pl.ds(k0, AW), pl.ds(col, per_n)], preferred_element_type=F32)
                return 0

            lax.fori_loop(0, DN * (C * AW // per_n), part, 0)

    def tiles(c, work):
        def one(i, _):
            base = pl.multiple_of(i * tile_rows, tile_rows)
            rows = pl.ds(base, tile_rows)
            for a in range(A):
                work(a, rows, pl.ds((a * C + c) * LANES, LANES), pl.ds(c * AW + a * LANES, LANES))
            return 0

        tile_rows = math.gcd(R, 64)
        lax.fori_loop(0, R // tile_rows, one, 0)

    def round_in(c):
        def work(a, rows, cols, inner):
            gath[0, d, c, a, rows, :] = amp[rows, cols].astype(BF16)
        tiles(c, work)

    def combine(c):
        def work(a, rows, cols, inner):
            onsite = coupling * occ[rows, cols].astype(F32) - center
            value = (onsite * amp[rows, cols] + ret_in[0, c, a, rows, :].astype(F32)
                     + dsum[rows, inner]) * 0.5
            first[rows, inner] = value
            gath[1, d, c, a, rows, :] = value.astype(BF16)
        tiles(c, work)

    def finish(c):
        def work(a, rows, cols, inner):
            onsite = coupling * occ[rows, cols].astype(F32) - center
            out[rows, cols] = (onsite * first[rows, inner] + ret_in[1, c, a, rows, :].astype(F32)
                               + dsum[rows, inner]) - amp[rows, cols]
        tiles(c, work)

    per_dev = R // blk

    def build_up():
        def one(i, _):
            a, rb = lax.div(i, per_dev), lax.rem(i, per_dev)
            row = (a * B + me_b) * per_dev + rb
            r0 = pl.multiple_of(rb * blk, blk)
            for j in range(A * B * R // LANES):
                tup[a, pl.ds(r0, blk), pl.ds(j * LANES, LANES)] = (
                    up_tab[0, up_map[row, 2 * j]] + up_tab[1, up_map[row, 2 * j + 1]])
            return 0
        lax.fori_loop(0, A * per_dev, one, 0)

    def build_down():
        two = LANES // blk

        def one(i, _):
            blocks = C * A
            src, rest = lax.div(i, blocks), lax.rem(i, blocks)
            c, a = lax.div(rest, A), lax.rem(rest, A)
            for h in range(two):
                col_block = (src * blocks + a * C + c) * two + h
                r0 = pl.multiple_of(i * LANES + h * blk, blk)
                for n in range(blocks):
                    nc, na = n // A, n % A
                    out_block = (d * blocks + na * C + nc) * two
                    tdn[pl.ds(r0, blk), pl.ds(n * LANES, LANES)] = (
                        down_tab[0, down_map[out_block, col_block]]
                        + down_tab[1, down_map[out_block + 1, col_block]])
            return 0
        lax.fori_loop(0, DN * C * A, one, 0)

    barrier = pltpu.get_barrier_semaphore()
    partners = ([(at_a(da) * B + me_b, d) for da in range(1, A)]
                + [(me_a * B + at_b(db), d) for db in range(1, B)]
                + [(u, at_x(dx) * 2 + me_k) for dx in range(1, X)]
                + [(u, me_x * 2 + 1 - me_k)])
    for dev in partners:
        pl.semaphore_signal(barrier, inc=1, device_id=dev, device_id_type=MESH)
    round_in(0)
    pl.semaphore_wait(barrier, len(partners))

    for c in range(C):
        if c:
            round_in(c)
        send_z(0, c)
        send_down(0, c)
    build_up()
    take_z(0, 0)
    take_x(0, 0)
    build_down()
    for c in range(C):
        if c:
            take_z(0, c)
            take_x(0, c)
        take_y(0, c)
        up_hop(0, c)
    for c in range(C):
        take_core(0, c)
    down_hop(0)
    for c in range(C):
        take_ret(0, c)
        combine(c)
        send_z(1, c)
        send_down(1, c)
    for c in range(C):
        take_z(1, c)
        take_x(1, c)
        take_y(1, c)
        up_hop(1, c)
    for c in range(C):
        take_core(1, c)
    down_hop(1)
    for c in range(C):
        take_ret(1, c)
        finish(c)
    for copy in sends:
        copy.wait_send()


def body(up_count, down_count, amplitudes, double_occ, up_cols, up_ids, up_blocks,
         down_cols, down_ids, down_blocks):
    R, W = amplitudes.shape
    shared, blk = up_blocks.shape[:2]
    total = up_cols.shape[0]
    A = math.gcd(4, up_count)
    B = up_count // A
    X = down_count // 2
    C = W // (A * LANES)

    def block_map(cols, ids):
        hit = cols[:, :, None] == jnp.arange(total, dtype=jnp.int32)[None, None, :]
        return jnp.sum(jnp.where(hit, ids[:, :, None] + 1, 0), axis=1)

    def table(blocks):
        low = jnp.pad(blocks, ((1, 0), (0, 0), (0, LANES - blk)))
        high = jnp.pad(blocks, ((1, 0), (0, 0), (LANES - blk, 0)))
        return jnp.stack([low, high])

    vmem = pl.BlockSpec(memory_space=pltpu.VMEM)
    smem = pl.BlockSpec(memory_space=pltpu.SMEM)
    dma = pltpu.SemaphoreType.DMA
    return pl.pallas_call(
        functools.partial(kernel, (A, B, X, C, R, blk)),
        out_shape=jax.ShapeDtypeStruct((R, W), F32),
        in_specs=[smem, smem, vmem, vmem, vmem, vmem],
        out_specs=vmem,
        scratch_shapes=[
            pltpu.VMEM((A, R, total * blk), BF16),
            pltpu.VMEM((total * blk, W), BF16),
            pltpu.VMEM((2, down_count, C, A, R, LANES), BF16),
            pltpu.VMEM((2, C, A, B, R, LANES), BF16),
            pltpu.VMEM((2, C, A, R, LANES), BF16),
            pltpu.VMEM((2, C, A, R, LANES), BF16),
            pltpu.VMEM((R, W), F32),
            pltpu.VMEM((R, W), F32),
            dma((2, C, A)), dma((2, C, A)),
            dma((2, C, A, B)), dma((2, C, A, B)),
            dma((2, C, A)), dma((2, C, A)),
            dma((2, C, X)), dma((2, C, X)),
            dma((2, C, X)), dma((2, C, X)),
        ],
        compiler_params=pltpu.CompilerParams(
            collective_id=0, has_side_effects=True, vmem_limit_bytes=60 * 2**20),
    )(block_map(up_cols, up_ids), block_map(down_cols, down_ids), amplitudes, double_occ,
      table(jnp.swapaxes(up_blocks, 1, 2)), table(down_blocks))


def solution(mesh):
    placed = (P("up", "down"), P("up", "down"), P(), P(), P(), P(), P(), P())
    return jax.shard_map(
        functools.partial(body, mesh.shape["up"], mesh.shape["down"]),
        mesh=mesh, in_specs=placed, out_specs=P("up", "down"), check_vma=False)
```
